32 devices in a mesh: outer: 8 (over z, core), inner: 4 (over y, x).
Axes of the slice: x: 2, y: 2, z: 4, core: 2. Of those that a mesh axis runs over, the one named last changes fastest.
Arguments:
- queries: bfloat16 [4096, 4096], P(('outer', 'inner')), may hold values from -8 to 8
- keys: bfloat16 [4096, 512], P(('outer', 'inner')), may hold values from -8 to 8
- values: bfloat16 [4096, 512], P(('outer', 'inner')), may hold values from -6 to 6
- acc_out: bfloat16 [4096, 4096], P(('outer', 'inner')), may hold values from -6 to 6
- acc_max: float32 [4096, 32], P(('outer', 'inner')), may hold values from 2 to 4
- acc_sum: float32 [4096, 32], P(('outer', 'inner')), may hold values from 16 to 256
- doc_lengths: int32 [16], replicated, may hold values from 1 to 2048, as said below
Outputs:
- new_out: bfloat16 [4096, 4096], P(('outer', 'inner'))
- new_max: float32 [4096, 32], P(('outer', 'inner'))
- new_sum: float32 [4096, 32], P(('outer', 'inner'))
The draws below stay inside these ranges and needn't reach their ends.
Inputs may be any that keep to these rules, and one draw needn't show every extreme that they name: `doc_lengths`: the lengths add up to 4096; one document is exactly 2048 long and none is longer.
All inputs are finite; a program needn't handle non-finite values.
Results may differ from the reference program's by a relative error of at most 0.0014.
Values may be sent and summed in bfloat16 or wider, within the bound.
No kernel may reach another device: no remote copies, remote signals or barrier semaphores. Data moves between devices by JAX's collectives and lax.ppermute only.
A program may use at most 64 MiB of HBM per device.

```python
import math
import jax
import jax.numpy as jnp
from jax import lax

TOK_DEV = 128
HQ = 32
KVH = 4
HD = 128
TOKENS = 4096
BLOCK = 512
DOCS = 16
DOC_MOST = 2048
N_OUTER = 8
N_INNER = 4


def draw_queries(key, part):
    group = HQ // KVH
    shape = (TOKENS, KVH, group, HD)
    result = jnp.clip(jax.random.normal(jax.random.fold_in(key, 1), shape, jnp.float32), -6.0, 6.0)
    return jnp.clip(result, -8.0, 8.0).reshape(TOKENS, HQ * HD).astype(jnp.bfloat16)


def draw_keys(key, part):
    shape = (TOKENS, KVH, HD)
    result = jnp.clip(jax.random.normal(jax.random.fold_in(key, 21), shape, jnp.float32), -6.0, 6.0)
    return jnp.clip(result, -8.0, 8.0).reshape(TOKENS, KVH * HD).astype(jnp.bfloat16)


def draw_doc_lengths(key, part):
    long_count = max(2, DOCS // 16)
    others = DOCS - long_count
    long_sizes = jax.random.randint(jax.random.fold_in(key, 32), (long_count - 1,), BLOCK // 2, 2 * BLOCK + 1).astype(jnp.int32)
    long_part = jnp.concatenate([jnp.full((1,), DOC_MOST, jnp.int32), long_sizes]).astype(jnp.int32)
    remain = (TOKENS - jnp.sum(long_part)).astype(jnp.int32)
    base_len = (remain // others).astype(jnp.int32)
    leftover = (remain - base_len * others).astype(jnp.int32)
    index_row = jnp.arange(others, dtype=jnp.int32)
    even_share = (base_len + (index_row < leftover).astype(jnp.int32)).astype(jnp.int32)
    pair_count = others // 2
    moving_amount = jax.random.randint(jax.random.fold_in(key, 31), (pair_count,), 0, base_len).astype(jnp.int32)
    changes = jnp.stack([moving_amount, -moving_amount], axis=1).reshape(2 * pair_count)
    changes = jnp.concatenate([changes, jnp.zeros((others - 2 * pair_count,), jnp.int32)]).astype(jnp.int32)
    short_part = (even_share + changes).astype(jnp.int32)
    combined = jnp.concatenate([long_part, short_part]).astype(jnp.int32)
    placing = jax.random.permutation(jax.random.fold_in(key, 33), DOCS)
    return jnp.zeros((DOCS,), jnp.int32).at[placing].set(combined).astype(jnp.int32)


def block_levels(key, shape, cuts, least, largest):
    factor_of, own = 1.0, jax.random.fold_in(key, 6)
    for position, blocks in cuts:
        heights = jnp.exp(jax.random.uniform(jax.random.fold_in(own, position), (blocks,), jnp.float32, least / len(cuts), largest / len(cuts)))
        factor_of = factor_of * jnp.repeat(heights, shape[position] // blocks).reshape([-1 if axis == position else 1 for axis in range(len(shape))])
    return factor_of


def scatter_about(stream_key, shape, scale, reach, pieces=(), kind=jnp.bfloat16):
    level = block_levels(stream_key, shape, pieces, -0.22, 0.18) if pieces else 1.0
    array = jax.random.normal(stream_key, shape, jnp.float32) * scale * level
    return jnp.minimum(jnp.maximum(array, -reach), reach).astype(kind)


def setup_inputs(seed: int = 0) -> dict:
    key_list = jax.random.split(jax.random.key(seed), 8)
    queries = draw_queries(jax.random.fold_in(key_list[7], 71), 0)
    keys = draw_keys(jax.random.fold_in(key_list[7], 71), 0)
    values = scatter_about(key_list[2], (TOKENS, KVH * HD), 1.0, 6.0, ((0, 32),))
    acc_out = scatter_about(key_list[3], (TOKENS, HQ * HD), 1.0, 6.0, ((0, 32),))
    acc_max = jnp.clip(2.0 + 2.0 * jax.random.uniform(key_list[4], (TOKENS, HQ), jnp.float32) ** block_levels(key_list[4], (TOKENS, HQ), ((0, 32),), -0.2, 0.2), 2.0, 4.0)
    acc_sum = jnp.clip(jnp.exp(math.log(256.0) - 2.7725887 * jax.random.uniform(key_list[5], (TOKENS, HQ), jnp.float32) ** block_levels(key_list[5], (TOKENS, HQ), ((0, 32),), -0.2, 0.2)), 16.0, 256.0)
    doc_lengths = draw_doc_lengths(jax.random.fold_in(key_list[7], 71), 0)
    return dict(queries=queries, keys=keys, values=values, acc_out=acc_out, acc_max=acc_max, acc_sum=acc_sum, doc_lengths=doc_lengths)


NEG = -1e+30

def reference(queries, keys, values, acc_out, acc_max, acc_sum, doc_lengths):
    group = HQ // KVH
    scale = 1.0 / math.sqrt(HD)
    ends = jnp.cumsum(doc_lengths).astype(jnp.int32)
    starts = (ends - doc_lengths).astype(jnp.int32)

    def tile(index):
        first = (index * TOK_DEV).astype(jnp.int32)
        k_block = ((index // N_INNER + N_OUTER - 1) % N_OUTER).astype(jnp.int32)
        k_first = (k_block * BLOCK).astype(jnp.int32)
        q_rows = lax.dynamic_slice_in_dim(queries, first, TOK_DEV, 0).astype(jnp.float32).reshape(TOK_DEV, KVH, group, HD)
        k_rows = lax.dynamic_slice_in_dim(keys, k_first, BLOCK, 0).astype(jnp.float32).reshape(BLOCK, KVH, HD)
        v_rows = lax.dynamic_slice_in_dim(values, k_first, BLOCK, 0).astype(jnp.float32).reshape(BLOCK, KVH, HD)
        qpos = first + jnp.arange(TOK_DEV, dtype=jnp.int32)
        kpos = k_first + jnp.arange(BLOCK, dtype=jnp.int32)
        qstart = lax.optimization_barrier(jnp.max(jnp.where(starts[None, :] <= qpos[:, None], starts[None, :], 0), axis=1))
        visible = (kpos[None, :] <= qpos[:, None]) & (kpos[None, :] >= qstart[:, None])
        keep = visible[:, None, None, :]
        scores = jnp.einsum('rhgd,nhd->rhgn', q_rows, k_rows) * scale
        scores = jnp.where(keep, scores, NEG)
        old_max = lax.dynamic_slice_in_dim(acc_max, first, TOK_DEV, 0).reshape(TOK_DEV, KVH, group)
        old_sum = lax.dynamic_slice_in_dim(acc_sum, first, TOK_DEV, 0).reshape(TOK_DEV, KVH, group)
        top = jnp.maximum(old_max, lax.optimization_barrier(jnp.max(scores, axis=-1)))
        weights = jnp.where(keep, jnp.exp(scores - top[..., None]), 0.0)
        kept = old_sum * jnp.exp(old_max - top)
        total = kept + lax.optimization_barrier(jnp.sum(weights, axis=-1))
        low = lax.optimization_barrier(weights.astype(jnp.bfloat16))
        mixed = jnp.einsum('rhgn,nhd->rhgd', low.astype(jnp.float32), v_rows)
        old_out = lax.dynamic_slice_in_dim(acc_out, first, TOK_DEV, 0).astype(jnp.float32).reshape(TOK_DEV, KVH, group, HD)
        result = (old_out * kept[..., None] + mixed) / total[..., None]
        return (result.reshape(TOK_DEV, HQ * HD).astype(jnp.bfloat16), top.reshape(TOK_DEV, HQ), total.reshape(TOK_DEV, HQ))
    outs = lax.map(tile, jnp.arange(TOKENS // TOK_DEV, dtype=jnp.int32))
    return (outs[0].reshape(TOKENS, HQ * HD), outs[1].reshape(TOKENS, HQ), outs[2].reshape(TOKENS, HQ))
```

```python
import functools
import math

import jax
import jax.numpy as jnp
from jax import lax
from jax.experimental import pallas as pl
from jax.experimental.pallas import tpu as pltpu
from jax.sharding import PartitionSpec as P

HD = 128
LANES = 128
HIDE = -1e30
LOG2E = math.log2(math.e)


def mask_kernel(block, docs, doc_ref, mine_ref, hide_ref):
    rows = mine_ref.shape[0]
    outer_at = lax.axis_index("outer")
    inner_at = lax.axis_index("inner")
    lane = lax.broadcasted_iota(jnp.int32, (8, LANES), 1)
    far = jnp.full((8, LANES), 2**30, jnp.int32)

    def one(d, state):
        first, starts, ends = state
        last = first + doc_ref[d]
        return last, jnp.where(lane == d, first, starts), jnp.where(lane == d, last, ends)

    unused, starts, ends = lax.fori_loop(0, docs, one, (jnp.int32(0), far, far))
    starts, ends = starts[:1], ends[:1]
    tok = lax.broadcasted_iota(jnp.int32, (rows, LANES), 0)
    qpos = tok + (outer_at * block + inner_at * rows)
    mine_ref[...] = jnp.where((starts <= qpos) & (qpos < ends), 1.0, 0.0).astype(jnp.bfloat16)
    for step in range(hide_ref.shape[0]):
        kpos = tok + ((outer_at - 1) * block + (inner_at ^ step) * rows)
        hide_ref[step] = jnp.where(kpos < starts, HIDE, 0.0).astype(jnp.bfloat16)


def attend_kernel(parts, kv_heads, group, scale, *refs):
    q_ref, old_ref, max_ref, sum_ref, mine_ref, hide_ref = refs[:6]
    kv_refs = refs[6 : 6 + parts]
    out_ref, new_max_ref, new_sum_ref, stage, sems = refs[6 + parts :]
    rows = q_ref.shape[0]
    heads = kv_heads * group
    wide = group * HD
    lane = lax.broadcasted_iota(jnp.int32, (rows, heads), 1)
    mine = mine_ref[...]
    ones = jnp.ones((parts * rows, HD), jnp.bfloat16)

    def one(h, unused):
        cols = pl.ds(pl.multiple_of(h * HD, HD), HD)
        vcols = pl.ds(pl.multiple_of((h + kv_heads) * HD, HD), HD)
        keys = jnp.concatenate(
            [jnp.concatenate([kv[:, cols], hide_ref[j]], axis=1) for j, kv in enumerate(kv_refs)], axis=0
        )
        vals = jnp.concatenate([jnp.concatenate([kv[:, vcols] for kv in kv_refs], axis=0), ones], axis=1)
        for g in range(group):
            head = h * group + g
            at = pl.ds(pl.multiple_of(head * HD, HD), HD)
            q = jnp.concatenate([q_ref[:, at], mine], axis=1)
            s = lax.dot_general(q, keys, (((1,), (1,)), ((), ())), preferred_element_type=jnp.float32)
            old_max = jnp.sum(jnp.where(lane == head, max_ref[...], 0.0), axis=1, keepdims=True)
            old_sum = jnp.sum(jnp.where(lane == head, sum_ref[...], 0.0), axis=1, keepdims=True)
            top = jnp.maximum(old_max, jnp.max(s, axis=1, keepdims=True) * scale)
            w = jnp.exp2(s * (scale * LOG2E) - top * LOG2E).astype(jnp.bfloat16)
            mixed = jnp.dot(w, vals, preferred_element_type=jnp.float32)
            kept = old_sum * jnp.exp2((old_max - top) * LOG2E)
            total = mixed[:, HD:] + kept
            result = (old_ref[:, at].astype(jnp.float32) * kept + mixed[:, :HD]) / total
            stage[:, at] = result.astype(jnp.bfloat16)
            new_max_ref[...] = jnp.where(lane == head, top, new_max_ref[...])
            new_sum_ref[...] = jnp.where(lane == head, total[:, :heads], new_sum_ref[...])
        span = pl.ds(pl.multiple_of(h * wide, wide), wide)
        pltpu.make_async_copy(stage.at[:, span], out_ref.at[:, span], sems.at[h]).start()
        return unused

    lax.fori_loop(0, kv_heads, one, 0)
    for h in range(kv_heads):
        span = pl.ds(h * wide, wide)
        pltpu.make_async_copy(stage.at[:, span], out_ref.at[:, span], sems.at[h]).wait()


def body(queries, keys, values, acc_out, acc_max, acc_sum, doc_lengths):
    rows = queries.shape[0]
    heads = acc_max.shape[1]
    kv_heads = keys.shape[1] // HD
    group = heads // kv_heads
    n_outer = lax.axis_size("outer")
    n_inner = lax.axis_size("inner")
    docs = doc_lengths.shape[0]
    vmem = pl.BlockSpec(memory_space=pltpu.VMEM)
    mine, hide = pl.pallas_call(
        functools.partial(mask_kernel, rows * n_inner, docs),
        out_shape=(
            jax.ShapeDtypeStruct((rows, LANES), jnp.bfloat16),
            jax.ShapeDtypeStruct((n_inner, rows, LANES), jnp.bfloat16),
        ),
        in_specs=[pl.BlockSpec(memory_space=pltpu.SMEM)],
        out_specs=(vmem, vmem),
    )(doc_lengths)
    both = jnp.concatenate([keys, values], axis=1)
    got = []
    for step in range(n_inner):
        pairs = [
            (o * n_inner + i, (o + 1) % n_outer * n_inner + (i ^ step))
            for o in range(n_outer)
            for i in range(n_inner)
        ]
        got.append(lax.ppermute(both, ("outer", "inner"), pairs))
    flops = 4 * rows * n_inner * rows * heads * HD
    return pl.pallas_call(
        functools.partial(attend_kernel, n_inner, kv_heads, group, 1.0 / math.sqrt(HD)),
        out_shape=(
            jax.ShapeDtypeStruct(queries.shape, jnp.bfloat16),
            jax.ShapeDtypeStruct((rows, heads), jnp.float32),
            jax.ShapeDtypeStruct((rows, heads), jnp.float32),
        ),
        in_specs=[vmem] * (6 + n_inner),
        out_specs=(pl.BlockSpec(memory_space=pl.ANY), vmem, vmem),
        scratch_shapes=[pltpu.VMEM(queries.shape, jnp.bfloat16), pltpu.SemaphoreType.DMA((kv_heads,))],
        compiler_params=pltpu.CompilerParams(vmem_limit_bytes=32 * 2**20),
        cost_estimate=pl.CostEstimate(flops=flops, bytes_accessed=4 * 2**20, transcendentals=0),
    )(queries, acc_out, acc_max, acc_sum, mine, hide, *got)


def solution(mesh):
    split = P(("outer", "inner"), None)
    return jax.shard_map(
        body,
        mesh=mesh,
        in_specs=(split,) * 6 + (P(),),
        out_specs=(split,) * 3,
        check_vma=False,
    )
```

```python
import functools
import math

import jax
import jax.numpy as jnp
from jax import lax
from jax.experimental import pallas as pl
from jax.experimental.pallas import tpu as pltpu
from jax.sharding import PartitionSpec as P

HD = 128
LANES = 128
HIDE = -1e30
LOG2E = math.log2(math.e)
VMEM = pl.BlockSpec(memory_space=pltpu.VMEM)
SMEM = pl.BlockSpec(memory_space=pltpu.SMEM)
PAIR = 2
PLAN = (
    ("0k", None, 0),
    ("0v", None, 0),
    ("1k", None, 1),
    ("2v", None, 2),
    ("1v", "0v", 1),
    ("2k", "0k", 2),
    ("3k", "1k", 2),
    ("3v", "2v", 1),
)
EARLY = (0,)
MASK_FLOPS = 2 * 10**10


def source(at, step, n_inner):
    return at ^ step if n_inner & (n_inner - 1) == 0 else lax.rem(at + step, n_inner)


def mask_kernel(steps, docs, doc_ref, mine_ref, hide_ref):
    rows = mine_ref.shape[0]
    n_inner = len(steps)
    outer_at = lax.axis_index("outer")
    inner_at = lax.axis_index("inner")
    lane = lax.broadcasted_iota(jnp.int32, (8, LANES), 1)
    far = jnp.full((8, LANES), 2**30, jnp.int32)

    def one(d, state):
        first, starts, ends = state
        last = first + doc_ref[d]
        return last, jnp.where(lane == d, first, starts), jnp.where(lane == d, last, ends)

    unused, starts, ends = lax.fori_loop(0, docs, one, (jnp.int32(0), far, far))
    tok = lax.broadcasted_iota(jnp.int32, (rows, LANES), 0)
    qpos = tok + (outer_at * n_inner + inner_at) * rows
    mine_ref[...] = jnp.where((starts[:1] <= qpos) & (qpos < ends[:1]), 1.0, 0.0).astype(jnp.bfloat16)
    for place, step in enumerate(steps):
        kpos = tok + ((outer_at - 1) * n_inner + source(inner_at, step, n_inner)) * rows
        hide_ref[pl.ds(place * rows, rows), :] = jnp.where(kpos < starts[:1], HIDE, 0.0).astype(jnp.bfloat16)


def rows_of(ref, heads):
    return jnp.concatenate([ref[pl.ds(x, 1), :] for x in heads], axis=1)


def work_of(kv_heads, group):
    return [(h, [h * group + g + k for k in range(PAIR)]) for h in range(kv_heads) for g in range(0, group, PAIR)]


def weigh_kernel(n_inner, early, kv_heads, group, scale, *refs):
    q_ref, old_ref, max_ref, sum_ref, mine_ref, hide_ref = refs[:6]
    k_refs = refs[6 : 6 + n_inner]
    v_refs = refs[6 + n_inner : 6 + n_inner + early]
    w_ref, acc_ref, top_ref, total_ref, inverse_ref = refs[6 + n_inner + early :]
    rows = q_ref.shape[0]
    split = early * rows
    work = work_of(kv_heads, group)

    def old_of(heads):
        return jnp.concatenate([old_ref[:, pl.ds(x * HD, HD)].T for x in heads], axis=1).astype(jnp.float32)

    def finish(heads, top, total, numer):
        inverse = 1.0 / total
        for k, x in enumerate(heads):
            cut = slice(k * rows, (k + 1) * rows)
            top_ref[pl.ds(x, 1), :] = top[:, cut]
            total_ref[pl.ds(x, 1), :] = total[:, cut]
            inverse_ref[pl.ds(x, 1), :] = inverse[:, cut]
            acc_ref[pl.ds(x * HD, HD), :] = numer[:, cut]

    live = lax.axis_index("outer") > 0

    @pl.when(live)
    def _():
        mine = jnp.concatenate([mine_ref[...]] * PAIR, axis=0)
        keys, vals = {}, {}

        def score(h, heads):
            if h not in keys:
                cols = pl.ds(h * HD, HD)
                keys[h] = jnp.concatenate([jnp.concatenate([k[:, cols] for k in k_refs], axis=0), hide_ref[...]], axis=1)
                vals[h] = jnp.concatenate([v[:, cols].T for v in v_refs], axis=1) if early else None
            q = jnp.concatenate([jnp.concatenate([q_ref[:, pl.ds(x * HD, HD)] for x in heads], axis=0), mine], axis=1)
            return lax.dot_general(keys[h], q, (((1,), (1,)), ((), ())), preferred_element_type=jnp.float32)

        def soften(s, heads):
            old_max = rows_of(max_ref, heads)
            top = jnp.maximum(old_max, jnp.max(s, axis=0, keepdims=True) * scale)
            w = jnp.exp2(s * (scale * LOG2E) - top * LOG2E)
            kept = rows_of(sum_ref, heads) * jnp.exp2((old_max - top) * LOG2E)
            total = kept + jnp.sum(w, axis=0, keepdims=True)
            w = w.astype(jnp.bfloat16)
            if split < w.shape[0]:
                w_ref[:, pl.ds(heads[0] * rows, len(heads) * rows)] = w[split:]
            return kept, top, total, w[:split]

        def mix(h, heads, kept, top, total, w):
            numer = old_of(heads) * kept
            if early:
                numer += jnp.dot(vals[h], w, preferred_element_type=jnp.float32)
            finish(heads, top, total, numer)

        scores, soft = {}, {}
        for t in range(len(work) + 2):
            if t < len(work):
                scores[t] = score(*work[t])
            if 0 <= t - 1 < len(work):
                soft[t - 1] = soften(scores.pop(t - 1), work[t - 1][1])
            if 0 <= t - 2 < len(work):
                mix(*work[t - 2], *soft.pop(t - 2))

    @pl.when(jnp.logical_not(live))
    def _():
        for h, heads in work:
            total = rows_of(sum_ref, heads)
            finish(heads, rows_of(max_ref, heads), total, old_of(heads) * total)


def mix_kernel(late, kv_heads, group, w_ref, acc_ref, inverse_ref, *refs):
    v_refs = refs[:late]
    out_ref, stage, sems = refs[late:]
    rows = out_ref.shape[0]
    wide = group * HD
    work = work_of(kv_heads, group)

    def flush(h):
        span = pl.ds(h * wide, wide)
        return pltpu.make_async_copy(stage.at[:, span], out_ref.at[:, span], sems.at[h])

    def finish(heads, numer):
        result = (numer * rows_of(inverse_ref, heads)).astype(jnp.bfloat16)
        for k, x in enumerate(heads):
            stage[:, pl.ds(x * HD, HD)] = result[:, k * rows : (k + 1) * rows].T
        if (heads[-1] + 1) % group == 0:
            flush(heads[0] // group).start()

    def numer_of(heads):
        return jnp.concatenate([acc_ref[pl.ds(x * HD, HD), :] for x in heads], axis=1)

    live = lax.axis_index("outer") > 0

    @pl.when(live)
    def _():
        vals = {}

        def mixed(h, heads):
            if h not in vals:
                cols = pl.ds(h * HD, HD)
                vals[h] = jnp.concatenate([v[:, cols].T for v in v_refs], axis=1)
            w = w_ref[:, pl.ds(heads[0] * rows, len(heads) * rows)]
            return jnp.dot(vals[h], w, preferred_element_type=jnp.float32)

        held = {}
        for t in range(len(work) + 1):
            if t < len(work):
                held[t] = mixed(*work[t])
            if t >= 1:
                heads = work[t - 1][1]
                finish(heads, numer_of(heads) + held.pop(t - 1))

    @pl.when(jnp.logical_not(live))
    def _():
        for h, heads in work:
            finish(heads, numer_of(heads))

    for h in range(kv_heads):
        flush(h).wait()


def move(keys, values, n_outer, n_inner):
    def direct(value, step):
        pairs = [
            (o * n_inner + source(i, step, n_inner), (o + 1) % n_outer * n_inner + i)
            for o in range(n_outer)
            for i in range(n_inner)
        ]
        return lax.ppermute(value, ("outer", "inner"), pairs)

    def within(value, step):
        return lax.ppermute(value, "inner", [(i ^ step, i) for i in range(n_inner)])

    own = {"k": keys, "v": values}
    got = {}
    if n_inner == 4:
        for piece, taken, step in PLAN:
            got[piece] = direct(own[piece[-1]], step) if taken is None else within(got[taken], step)
    else:
        for step in range(n_inner):
            for kind in "kv":
                got[f"{step}{kind}"] = direct(own[kind], step)
    return got


def body(queries, keys, values, acc_out, acc_max, acc_sum, doc_lengths):
    rows, width = queries.shape
    heads = acc_max.shape[1]
    kv_heads = keys.shape[1] // HD
    group = heads // kv_heads
    n_outer = lax.axis_size("outer")
    n_inner = lax.axis_size("inner")
    early = EARLY if n_inner == 4 else tuple(range(n_inner // 2))
    steps = early + tuple(step for step in range(n_inner) if step not in early)
    got = move(keys, values, n_outer, n_inner)
    mine, hide = pl.pallas_call(
        functools.partial(mask_kernel, steps, doc_lengths.shape[0]),
        out_shape=(
            jax.ShapeDtypeStruct((rows, LANES), jnp.bfloat16),
            jax.ShapeDtypeStruct((n_inner * rows, LANES), jnp.bfloat16),
        ),
        in_specs=[SMEM],
        out_specs=(VMEM,) * 2,
        compiler_params=pltpu.CompilerParams(vmem_limit_bytes=2 * 2**20),
        cost_estimate=pl.CostEstimate(flops=MASK_FLOPS, bytes_accessed=2**18, transcendentals=0),
    )(doc_lengths)
    late = n_inner - len(early)
    stat = jax.ShapeDtypeStruct((heads, rows), jnp.float32)
    area = rows * rows * heads
    w, acc, top, total, inverse = pl.pallas_call(
        functools.partial(weigh_kernel, n_inner, len(early), kv_heads, group, 1.0 / math.sqrt(HD)),
        out_shape=(
            jax.ShapeDtypeStruct((late * rows, heads * rows), jnp.bfloat16),
            jax.ShapeDtypeStruct((width, rows), jnp.float32),
            stat,
            stat,
            stat,
        ),
        in_specs=[VMEM] * (6 + n_inner + len(early)),
        out_specs=(VMEM,) * 5,
        compiler_params=pltpu.CompilerParams(vmem_limit_bytes=16 * 2**20),
        cost_estimate=pl.CostEstimate(
            flops=2 * area * HD * (n_inner + len(early)), bytes_accessed=2**20, transcendentals=area * n_inner
        ),
    )(
        queries,
        acc_out,
        acc_max.T,
        acc_sum.T,
        mine,
        hide,
        *[got[f"{step}k"] for step in steps],
        *[got[f"{step}v"] for step in early],
    )
    out = pl.pallas_call(
        functools.partial(mix_kernel, late, kv_heads, group),
        out_shape=jax.ShapeDtypeStruct((rows, width), jnp.bfloat16),
        in_specs=[VMEM] * (3 + late),
        out_specs=pl.BlockSpec(memory_space=pl.ANY),
        scratch_shapes=[pltpu.VMEM((rows, width), jnp.bfloat16), pltpu.SemaphoreType.DMA((kv_heads,))],
        compiler_params=pltpu.CompilerParams(vmem_limit_bytes=16 * 2**20),
        cost_estimate=pl.CostEstimate(flops=2 * area * HD * late, bytes_accessed=2**20, transcendentals=0),
    )(w, acc, inverse, *[got[f"{step}v"] for step in steps[len(early) :]])
    return out, top.T, total.T


def solution(mesh):
    split = P(("outer", "inner"), None)
    return jax.shard_map(
        body,
        mesh=mesh,
        in_specs=(split,) * 6 + (P(),),
        out_specs=(split,) * 3,
        check_vma=False,
    )
```

```python
import functools
import math

import jax
import jax.numpy as jnp
from jax import lax
from jax.experimental import pallas as pl
from jax.experimental.pallas import tpu as pltpu
from jax.sharding import PartitionSpec as P

HD = 128
LANES = 128
HIDE = -1e30
LOG2E = math.log2(math.e)
VMEM = pl.BlockSpec(memory_space=pltpu.VMEM)
SMEM = pl.BlockSpec(memory_space=pltpu.SMEM)
PAIR = 1
MIX_PAIR = 2
FLUSH = 8
PLAN = (
    (("0k",), (), 0),
    (("1k",), (), 1),
    (("2k",), (), 2),
    (("0v",), (), 0),
    (("2v",), (), 2),
    (("3k",), ("1k",), 2),
    (("1v", "3v"), ("0v", "2v"), 1),
)
STAGES = ((0, 1), (2,), (3,))
EARLY = ()
TIES = {}
AHEAD_FLOPS = 2 * 10**10


def source(at, step, n_inner):
    return at ^ step if n_inner & (n_inner - 1) == 0 else lax.rem(at + step, n_inner)


def ahead_kernel(out_ref):
    out_ref[...] = jnp.zeros_like(out_ref)


def masks(steps, n_inner, doc_ref, mine_ref, hide_refs):
    rows = mine_ref.shape[0]
    outer_at = lax.axis_index("outer")
    inner_at = lax.axis_index("inner")
    lane = lax.broadcasted_iota(jnp.int32, (8, LANES), 1)
    far = jnp.full((8, LANES), 2**30, jnp.int32)

    def one(d, state):
        first, starts, ends = state
        last = first + doc_ref[d]
        return last, jnp.where(lane == d, first, starts), jnp.where(lane == d, last, ends)

    unused, starts, ends = lax.fori_loop(0, doc_ref.shape[0], one, (jnp.int32(0), far, far), unroll=4)
    tok = lax.broadcasted_iota(jnp.int32, (rows, LANES), 0)
    qpos = tok + (outer_at * n_inner + inner_at) * rows
    mine_ref[...] = jnp.where((starts[:1] <= qpos) & (qpos < ends[:1]), 1.0, 0.0).astype(jnp.bfloat16)
    for hide_ref, held in zip(hide_refs, steps):
        for place, step in enumerate(held):
            kpos = tok + ((outer_at - 1) * n_inner + source(inner_at, step, n_inner)) * rows
            hide_ref[pl.ds(place * rows, rows), :] = jnp.where(kpos < starts[:1], HIDE, 0.0).astype(jnp.bfloat16)


def rows_of(ref, heads):
    return jnp.concatenate([ref[pl.ds(x, 1), :] for x in heads], axis=1)


def work_of(kv_heads, group, pair):
    return [(h, [h * group + g + k for k in range(pair)]) for h in range(kv_heads) for g in range(0, group, pair)]


def weigh_kernel(stages, at, n_inner, early, k_at, v_at, kv_heads, group, scale, *refs):
    begin, end = at == 0, at + 1 == len(stages)
    refs = list(refs)
    if begin:
        doc_ref, unused, old_ref = refs[:3]
        mine_ref, hide_ref = refs[-2:]
        refs = refs[3:-2]
    else:
        mine_ref, hide_ref = refs[:2]
        refs = refs[2:]
    q_ref, max_ref, sum_ref = refs[:3]
    rows = q_ref.shape[0]
    k_refs = [refs[3 + which].at[pl.ds(first, rows)] for which, first in k_at]
    v_refs = [refs[3 + which].at[pl.ds(first, rows)] for which, first in v_at]
    refs = refs[3 + 1 + max(which for which, first in k_at + v_at) :]
    w_ref, top_ref, total_ref = refs[:3]
    refs = refs[3:]
    if end:
        inverse_ref = refs.pop(0)
    if not begin:
        shrink_ref = refs.pop(0)
    if begin:
        acc_ref = refs.pop(0)
        if len(stages) > 1:
            later_mine_ref, later_refs = refs[0], refs[1:]
    split = early * rows
    work = work_of(kv_heads, group, PAIR)
    live = lax.axis_index("outer") > 0

    def finish(heads, top, total, shrink, numer):
        inverse = 1.0 / total if end else None
        for k, x in enumerate(heads):
            cut = slice(k * rows, (k + 1) * rows)
            top_ref[pl.ds(x, 1), :] = top[:, cut]
            total_ref[pl.ds(x, 1), :] = total[:, cut]
            if end:
                inverse_ref[pl.ds(x, 1), :] = inverse[:, cut]
            if begin:
                acc_ref[pl.ds(x * HD, HD), :] = numer[:, cut]
            else:
                shrink_ref[pl.ds(x, 1), :] = shrink[:, cut]

    def old_of(heads):
        return jnp.concatenate([old_ref[:, pl.ds(x * HD, HD)].T for x in heads], axis=1).astype(jnp.float32)

    @pl.when(live)
    def _():
        if begin:
            masks(stages, n_inner, doc_ref, mine_ref, [hide_ref] + list(later_refs if len(stages) > 1 else []))
            if len(stages) > 1:
                later_mine_ref[...] = mine_ref[...]
        mine = jnp.concatenate([mine_ref[...]] * PAIR, axis=0)
        keys, vals = {}, {}

        def score(h, heads):
            if h not in keys:
                cols = pl.ds(h * HD, HD)
                keys[h] = jnp.concatenate([jnp.concatenate([k[:, cols] for k in k_refs], axis=0), hide_ref[...]], axis=1)
                vals[h] = jnp.concatenate([v[:, cols].T for v in v_refs], axis=1) if early else None
            q = jnp.concatenate([jnp.concatenate([q_ref[:, pl.ds(x * HD, HD)] for x in heads], axis=0), mine], axis=1)
            return lax.dot_general(keys[h], q, (((1,), (1,)), ((), ())), preferred_element_type=jnp.float32)

        def soften(s, heads):
            old_max = rows_of(max_ref, heads)
            top = jnp.maximum(old_max, jnp.max(s, axis=0, keepdims=True) * scale)
            w = jnp.exp2(s * (scale * LOG2E) - top * LOG2E)
            shrink = jnp.exp2((old_max - top) * LOG2E)
            kept = rows_of(sum_ref, heads) * shrink
            total = kept + jnp.sum(w, axis=0, keepdims=True)
            w = w.astype(jnp.bfloat16)
            if split < w.shape[0]:
                w_ref[:, pl.ds(heads[0] * rows, len(heads) * rows)] = w[split:]
            return kept, top, total, shrink, w[:split]

        def mix(h, heads, kept, top, total, shrink, w):
            numer = old_of(heads) * kept if begin else None
            if early:
                numer += jnp.dot(vals[h], w, preferred_element_type=jnp.float32)
            finish(heads, top, total, shrink, numer)

        scores, soft = {}, {}
        for t in range(len(work) + 2):
            if t < len(work):
                scores[t] = score(*work[t])
            if 0 <= t - 1 < len(work):
                soft[t - 1] = soften(scores.pop(t - 1), work[t - 1][1])
            if 0 <= t - 2 < len(work):
                mix(*work[t - 2], *soft.pop(t - 2))

    @pl.when(jnp.logical_not(live))
    def _():
        for h, heads in work:
            total = rows_of(sum_ref, heads)
            numer = old_of(heads) * total if begin else None
            finish(heads, rows_of(max_ref, heads), total, jnp.ones_like(total), numer)


def mix_kernel(stages, v_at, kv_heads, group, *refs):
    out_ref, top_out, total_out, stage, sems, stat_sems = refs[-6:]
    top_ref, total_ref = refs[:2]
    refs = refs[2:]
    rows = out_ref.shape[0]
    count = len(v_at)
    stats = [
        pltpu.make_async_copy(top_ref, top_out, stat_sems.at[0]),
        pltpu.make_async_copy(total_ref, total_out, stat_sems.at[1]),
    ]
    for copy in stats:
        copy.start()
    w_refs, shrink_refs = refs[:count], refs[count : 2 * count - 1]
    acc_ref, inverse_ref = refs[2 * count - 1 : 2 * count + 1]
    refs = refs[2 * count + 1 :]
    v_refs = [[refs[which].at[pl.ds(first, rows)] for which, first in held] for held in v_at]
    wide = FLUSH * HD
    work = work_of(kv_heads, group, MIX_PAIR)

    def flush(h):
        span = pl.ds(h * wide, wide)
        return pltpu.make_async_copy(stage.at[:, span], out_ref.at[:, span], sems.at[h])

    def finish(heads, numer):
        result = (numer * rows_of(inverse_ref, heads)).astype(jnp.bfloat16)
        for k, x in enumerate(heads):
            stage[:, pl.ds(x * HD, HD)] = result[:, k * rows : (k + 1) * rows].T
        if (heads[-1] + 1) % FLUSH == 0:
            flush(heads[-1] // FLUSH).start()

    def numer_of(heads):
        return jnp.concatenate([acc_ref[pl.ds(x * HD, HD), :] for x in heads], axis=1)

    live = lax.axis_index("outer") > 0

    @pl.when(live)
    def _():
        vals = {}

        def mixed(h, heads):
            if h not in vals:
                cols = pl.ds(h * HD, HD)
                vals[h] = [jnp.concatenate([v[:, cols].T for v in held], axis=1) if held else None for held in v_refs]
            at = pl.ds(heads[0] * rows, len(heads) * rows)
            return [
                jnp.dot(v, w[:, at], preferred_element_type=jnp.float32) if v is not None else None
                for v, w in zip(vals[h], w_refs)
            ]

        def close(heads, parts):
            numer = numer_of(heads)
            for at, part in enumerate(parts):
                if part is not None:
                    numer = numer + part
                if at + 1 < len(parts):
                    numer = numer * rows_of(shrink_refs[at], heads)
            finish(heads, numer)

        held = {}
        for t in range(len(work) + 1):
            if t < len(work):
                held[t] = mixed(*work[t])
            if t >= 1:
                close(work[t - 1][1], held.pop(t - 1))

    @pl.when(jnp.logical_not(live))
    def _():
        for h, heads in work:
            finish(heads, numer_of(heads))

    for h in range(kv_heads * group // FLUSH):
        flush(h).wait()
    for copy in stats:
        copy.wait()


def move(keys, values, n_outer, n_inner):
    def direct(value, step):
        pairs = [
            (o * n_inner + (source(i, step, n_inner) if o + 1 < n_outer else i), (o + 1) % n_outer * n_inner + i)
            for o in range(n_outer)
            for i in range(n_inner)
        ]
        return lax.ppermute(value, ("outer", "inner"), pairs)

    def within(value, step):
        return lax.ppermute(value, "inner", [(i ^ step, i) for i in range(n_inner)])

    own = {"k": keys, "v": values}
    rows = keys.shape[0]
    got = {}
    if n_inner == 4:
        plan = PLAN
    else:
        plan = [((f"{step}{kind}",), (), step) for kind in "kv" for step in range(n_inner)]
    for pieces, taken, step in plan:
        after = [x for x in TIES.get(pieces[0], ()) if n_inner == 4]
        if taken:
            parts = [got[x][0][got[x][1] : got[x][1] + rows] if got[x][0].shape[0] > rows else got[x][0] for x in taken]
            sent = jnp.concatenate(parts, axis=0) if len(parts) > 1 else parts[0]
        else:
            sent = own[pieces[0][-1]]
        if after:
            held = lax.optimization_barrier((sent, *[got[x][0] for x in after]))
            sent = held[0]
            for x, array in zip(after, held[1:]):
                got[x] = (array, got[x][1])
        moved = within(sent, step) if taken else direct(sent, step)
        for place, piece in enumerate(pieces):
            got[piece] = (moved, place * rows)
    return got


def gather(got, pieces):
    arrays, at = [], []
    for piece in pieces:
        array, first = got[piece]
        which = next((n for n, known in enumerate(arrays) if known is array), len(arrays))
        if which == len(arrays):
            arrays.append(array)
        at.append((which, first))
    return arrays, at


def body(queries, keys, values, acc_out, acc_max, acc_sum, doc_lengths):
    rows, width = queries.shape
    heads = acc_max.shape[1]
    kv_heads = keys.shape[1] // HD
    group = heads // kv_heads
    n_outer = lax.axis_size("outer")
    n_inner = lax.axis_size("inner")
    if n_inner == 4:
        stages, early = STAGES, EARLY
    else:
        half = n_inner // 2
        stages, early = (tuple(range(half)), tuple(range(half, n_inner))), ()
    got = move(keys, values, n_outer, n_inner)
    ahead = pl.pallas_call(
        ahead_kernel,
        out_shape=jax.ShapeDtypeStruct((8, LANES), jnp.float32),
        out_specs=VMEM,
        compiler_params=pltpu.CompilerParams(vmem_limit_bytes=2**20),
        cost_estimate=pl.CostEstimate(flops=AHEAD_FLOPS, bytes_accessed=4096, transcendentals=0),
    )()
    stat = jax.ShapeDtypeStruct((heads, rows), jnp.float32)
    area = rows * rows * heads
    tile = jax.ShapeDtypeStruct((rows, LANES), jnp.bfloat16)

    def hide_of(steps):
        return jax.ShapeDtypeStruct((len(steps) * rows, LANES), jnp.bfloat16)

    ws, shrinks, late = [], [], []
    top, total = acc_max.T, acc_sum.T
    for at, steps in enumerate(stages):
        begin, end = at == 0, at + 1 == len(stages)
        now = early if begin else ()
        late.append([step for step in steps if step not in now])
        arrays, places = gather(got, [f"{step}k" for step in steps] + [f"{step}v" for step in now])
        operands = [doc_lengths, ahead, acc_out] if begin else [mine, hides[at - 1]]
        operands += [queries, top, total, *arrays]
        out_shape = [jax.ShapeDtypeStruct((max(1, len(late[-1])) * rows, heads * rows), jnp.bfloat16), stat, stat]
        out_shape += [stat] * ((not begin) + end)
        if begin:
            out_shape.append(jax.ShapeDtypeStruct((width, rows), jnp.float32))
            out_shape += [tile] + [hide_of(steps) for steps in stages[1:]] if not end else []
        outs = pl.pallas_call(
            functools.partial(
                weigh_kernel,
                stages,
                at,
                n_inner,
                len(now),
                places[: len(steps)],
                places[len(steps) :],
                kv_heads,
                group,
                1.0 / math.sqrt(HD),
            ),
            out_shape=tuple(out_shape),
            in_specs=([SMEM] if begin else [VMEM]) + [VMEM] * (len(operands) - 1),
            out_specs=(VMEM,) * len(out_shape),
            scratch_shapes=[pltpu.VMEM(x.shape, x.dtype) for x in (tile, hide_of(steps))] if begin else [],
            compiler_params=pltpu.CompilerParams(vmem_limit_bytes=12 * 2**20),
            cost_estimate=pl.CostEstimate(
                flops=2 * area * HD * (len(steps) + len(now)), bytes_accessed=2**20, transcendentals=area * len(steps)
            ),
        )(*operands)
        outs = list(outs)
        ws.append(outs[0])
        top, total = outs[1:3]
        outs = outs[3:]
        if end:
            inverse = outs.pop(0)
        if not begin:
            shrinks.append(outs.pop(0))
        else:
            acc = outs.pop(0)
            mine, hides = (outs[0], outs[1:]) if not end else (None, None)
    arrays, places = gather(got, [f"{step}v" for held in late for step in held])
    places = iter(places)
    v_at = [[next(places) for step in held] for held in late]
    out, top, total = pl.pallas_call(
        functools.partial(mix_kernel, stages, v_at, kv_heads, group),
        out_shape=(jax.ShapeDtypeStruct((rows, width), jnp.bfloat16), stat, stat),
        in_specs=[VMEM] * (2 * len(stages) + 3 + len(arrays)),
        out_specs=(pl.BlockSpec(memory_space=pl.ANY),) * 3,
        scratch_shapes=[
            pltpu.VMEM((rows, width), jnp.bfloat16),
            pltpu.SemaphoreType.DMA((heads // FLUSH,)),
            pltpu.SemaphoreType.DMA((2,)),
        ],
        compiler_params=pltpu.CompilerParams(vmem_limit_bytes=12 * 2**20),
        cost_estimate=pl.CostEstimate(flops=2 * area * HD * n_inner, bytes_accessed=2**20, transcendentals=0),
    )(top, total, *ws, *shrinks, acc, inverse, *arrays)
    return out, top.T, total.T


def solution(mesh):
    split = P(("outer", "inner"), None)
    return jax.shard_map(
        body,
        mesh=mesh,
        in_specs=(split,) * 6 + (P(),),
        out_specs=(split,) * 3,
        check_vma=False,
    )
```

```python
import functools
import math

import jax
import jax.numpy as jnp
from jax import lax
from jax.experimental import pallas as pl
from jax.experimental.pallas import tpu as pltpu
from jax.sharding import PartitionSpec as P

HD = 128
LANES = 128
HIDE = -1e30
LOG2E = math.log2(math.e)
VMEM = pl.BlockSpec(memory_space=pltpu.VMEM)
SMEM = pl.BlockSpec(memory_space=pltpu.SMEM)
PAIR = 1
MIX_PAIR = 2
FLUSH = 8
PLAN = (
    (("0k",), (), 0),
    (("1k",), (), 1),
    (("2k",), (), 2),
    (("0v",), (), 0),
    (("2v",), (), 2),
    (("3k",), ("1k",), 2),
    (("1v", "3v"), ("0v", "2v"), 1),
)
STAGES = ((0, 1), (2,), (3,))
EARLY = ()
TIES = {}
AHEAD_FLOPS = 2 * 10**10


def source(at, step, n_inner):
    return at ^ step if n_inner & (n_inner - 1) == 0 else lax.rem(at + step, n_inner)


def ahead_kernel(out_ref):
    out_ref[...] = jnp.zeros_like(out_ref)


def masks(steps, n_inner, doc_ref, mine_ref, hide_refs):
    rows = mine_ref.shape[0]
    outer_at = lax.axis_index("outer")
    inner_at = lax.axis_index("inner")
    lane = lax.broadcasted_iota(jnp.int32, (8, LANES), 1)
    far = jnp.full((8, LANES), 2**30, jnp.int32)

    def one(d, state):
        first, starts, ends = state
        last = first + doc_ref[d]
        return last, jnp.where(lane == d, first, starts), jnp.where(lane == d, last, ends)

    unused, starts, ends = lax.fori_loop(0, doc_ref.shape[0], one, (jnp.int32(0), far, far), unroll=4)
    tok = lax.broadcasted_iota(jnp.int32, (rows, LANES), 0)
    qpos = tok + (outer_at * n_inner + inner_at) * rows
    mine_ref[...] = jnp.where((starts[:1] <= qpos) & (qpos < ends[:1]), 1.0, 0.0).astype(jnp.bfloat16)
    for hide_ref, held in zip(hide_refs, steps):
        for place, step in enumerate(held):
            kpos = tok + ((outer_at - 1) * n_inner + source(inner_at, step, n_inner)) * rows
            hide_ref[pl.ds(place * rows, rows), :] = jnp.where(kpos < starts[:1], HIDE, 0.0).astype(jnp.bfloat16)


def rows_of(ref, heads):
    return jnp.concatenate([ref[pl.ds(x, 1), :] for x in heads], axis=1)


def work_of(kv_heads, group, pair):
    return [(h, [h * group + g + k for k in range(pair)]) for h in range(kv_heads) for g in range(0, group, pair)]


def weigh_kernel(stages, at, n_inner, early, k_at, v_at, kv_heads, group, scale, *refs):
    begin, end = at == 0, at + 1 == len(stages)
    refs = list(refs)
    if begin:
        doc_ref, unused, old_ref = refs[:3]
        mine_ref, hide_ref = refs[-3:-1]
        refs = refs[3:-3] + refs[-1:]
    else:
        mine_ref, hide_ref = refs[:2]
        refs = refs[2:]
    q_ref, max_ref, sum_ref = refs[:3]
    rows = q_ref.shape[0]
    k_refs = [refs[3 + which].at[pl.ds(first, rows)] for which, first in k_at]
    v_refs = [refs[3 + which].at[pl.ds(first, rows)] for which, first in v_at]
    refs = refs[3 + 1 + max(which for which, first in k_at + v_at) :]
    w_ref, top_ref, total_ref = refs[:3]
    refs = refs[3:]
    if end:
        inverse_ref = refs.pop(0)
    if not begin:
        shrink_ref = refs.pop(0)
    if begin:
        acc_ref, *rest_refs = refs[:4]
        rest_sems, refs = refs[-1], refs[4:-1]
        if len(stages) > 1:
            later_mine_ref, later_refs = refs[0], refs[1:]
    split = early * rows
    work = work_of(kv_heads, group, PAIR)
    live = lax.axis_index("outer") > 0

    def finish(heads, top, total, shrink, numer):
        inverse = 1.0 / total if end else None
        for k, x in enumerate(heads):
            cut = slice(k * rows, (k + 1) * rows)
            top_ref[pl.ds(x, 1), :] = top[:, cut]
            total_ref[pl.ds(x, 1), :] = total[:, cut]
            if end:
                inverse_ref[pl.ds(x, 1), :] = inverse[:, cut]
            if begin:
                acc_ref[pl.ds(x * HD, HD), :] = numer[:, cut]
            else:
                shrink_ref[pl.ds(x, 1), :] = shrink[:, cut]

    def old_of(heads):
        return jnp.concatenate([old_ref[:, pl.ds(x * HD, HD)].T for x in heads], axis=1).astype(jnp.float32)

    @pl.when(live)
    def _():
        if begin:
            masks(stages, n_inner, doc_ref, mine_ref, [hide_ref] + list(later_refs if len(stages) > 1 else []))
            if len(stages) > 1:
                later_mine_ref[...] = mine_ref[...]
        mine = jnp.concatenate([mine_ref[...]] * PAIR, axis=0)
        keys, vals = {}, {}

        def score(h, heads):
            if h not in keys:
                cols = pl.ds(h * HD, HD)
                keys[h] = jnp.concatenate([jnp.concatenate([k[:, cols] for k in k_refs], axis=0), hide_ref[...]], axis=1)
                vals[h] = jnp.concatenate([v[:, cols].T for v in v_refs], axis=1) if early else None
            q = jnp.concatenate([jnp.concatenate([q_ref[:, pl.ds(x * HD, HD)] for x in heads], axis=0), mine], axis=1)
            return lax.dot_general(keys[h], q, (((1,), (1,)), ((), ())), preferred_element_type=jnp.float32)

        def soften(s, heads):
            old_max = rows_of(max_ref, heads)
            top = jnp.maximum(old_max, jnp.max(s, axis=0, keepdims=True) * scale)
            w = jnp.exp2(s * (scale * LOG2E) - top * LOG2E)
            shrink = jnp.exp2((old_max - top) * LOG2E)
            kept = rows_of(sum_ref, heads) * shrink
            total = kept + jnp.sum(w, axis=0, keepdims=True)
            w = w.astype(jnp.bfloat16)
            if split < w.shape[0]:
                w_ref[:, pl.ds(heads[0] * rows, len(heads) * rows)] = w[split:]
            return kept, top, total, shrink, w[:split]

        def mix(h, heads, kept, top, total, shrink, w):
            numer = old_of(heads) * kept if begin else None
            if early:
                numer += jnp.dot(vals[h], w, preferred_element_type=jnp.float32)
            finish(heads, top, total, shrink, numer)

        scores, soft = {}, {}
        for t in range(len(work) + 2):
            if t < len(work):
                scores[t] = score(*work[t])
            if 0 <= t - 1 < len(work):
                soft[t - 1] = soften(scores.pop(t - 1), work[t - 1][1])
            if 0 <= t - 2 < len(work):
                mix(*work[t - 2], *soft.pop(t - 2))

    @pl.when(jnp.logical_not(live))
    def _():
        if begin:
            copies = [
                pltpu.make_async_copy(ref, rest, rest_sems.at[n])
                for n, (ref, rest) in enumerate(zip((old_ref, max_ref, sum_ref), rest_refs))
            ]
            for copy in copies:
                copy.start()
        top_ref[...] = max_ref[...]
        total_ref[...] = sum_ref[...]
        if begin:
            for copy in copies:
                copy.wait()


def mix_kernel(stages, v_at, kv_heads, group, *refs):
    out_ref, top_out, total_out, stage, sems, stat_sems = refs[-6:]
    top_ref, total_ref = refs[3:5]
    refs = refs[5:]
    rows = out_ref.shape[0]
    count = len(v_at)
    stats = [
        pltpu.make_async_copy(top_ref, top_out, stat_sems.at[0]),
        pltpu.make_async_copy(total_ref, total_out, stat_sems.at[1]),
    ]
    w_refs, shrink_refs = refs[:count], refs[count : 2 * count - 1]
    acc_ref, inverse_ref = refs[2 * count - 1 : 2 * count + 1]
    refs = refs[2 * count + 1 :]
    v_refs = [[refs[which].at[pl.ds(first, rows)] for which, first in held] for held in v_at]
    wide = FLUSH * HD
    work = work_of(kv_heads, group, MIX_PAIR)

    def flush(h):
        span = pl.ds(h * wide, wide)
        return pltpu.make_async_copy(stage.at[:, span], out_ref.at[:, span], sems.at[h])

    def finish(heads, numer):
        result = (numer * rows_of(inverse_ref, heads)).astype(jnp.bfloat16)
        for k, x in enumerate(heads):
            stage[:, pl.ds(x * HD, HD)] = result[:, k * rows : (k + 1) * rows].T
        if (heads[-1] + 1) % FLUSH == 0:
            flush(heads[-1] // FLUSH).start()

    def numer_of(heads):
        return jnp.concatenate([acc_ref[pl.ds(x * HD, HD), :] for x in heads], axis=1)

    @pl.when(lax.axis_index("outer") > 0)
    def _():
        for copy in stats:
            copy.start()
        vals = {}

        def mixed(h, heads):
            if h not in vals:
                cols = pl.ds(h * HD, HD)
                vals[h] = [jnp.concatenate([v[:, cols].T for v in held], axis=1) if held else None for held in v_refs]
            at = pl.ds(heads[0] * rows, len(heads) * rows)
            return [
                jnp.dot(v, w[:, at], preferred_element_type=jnp.float32) if v is not None else None
                for v, w in zip(vals[h], w_refs)
            ]

        def close(heads, parts):
            numer = numer_of(heads)
            for at, part in enumerate(parts):
                if part is not None:
                    numer = numer + part
                if at + 1 < len(parts):
                    numer = numer * rows_of(shrink_refs[at], heads)
            finish(heads, numer)

        held = {}
        for t in range(len(work) + 1):
            if t < len(work):
                held[t] = mixed(*work[t])
            if t >= 1:
                close(work[t - 1][1], held.pop(t - 1))

        for h in range(kv_heads * group // FLUSH):
            flush(h).wait()
        for copy in stats:
            copy.wait()


def move(keys, values, n_outer, n_inner):
    def direct(value, step):
        pairs = [
            (o * n_inner + (source(i, step, n_inner) if o + 1 < n_outer else i), (o + 1) % n_outer * n_inner + i)
            for o in range(n_outer)
            for i in range(n_inner)
        ]
        return lax.ppermute(value, ("outer", "inner"), pairs)

    def within(value, step):
        return lax.ppermute(value, "inner", [(i ^ step, i) for i in range(n_inner)])

    own = {"k": keys, "v": values}
    rows = keys.shape[0]
    got = {}
    if n_inner == 4:
        plan = PLAN
    else:
        plan = [((f"{step}{kind}",), (), step) for kind in "kv" for step in range(n_inner)]
    for pieces, taken, step in plan:
        after = [x for x in TIES.get(pieces[0], ()) if n_inner == 4]
        if taken:
            parts = [got[x][0][got[x][1] : got[x][1] + rows] if got[x][0].shape[0] > rows else got[x][0] for x in taken]
            sent = jnp.concatenate(parts, axis=0) if len(parts) > 1 else parts[0]
        else:
            sent = own[pieces[0][-1]]
        if after:
            held = lax.optimization_barrier((sent, *[got[x][0] for x in after]))
            sent = held[0]
            for x, array in zip(after, held[1:]):
                got[x] = (array, got[x][1])
        moved = within(sent, step) if taken else direct(sent, step)
        for place, piece in enumerate(pieces):
            got[piece] = (moved, place * rows)
    return got


def gather(got, pieces):
    arrays, at = [], []
    for piece in pieces:
        array, first = got[piece]
        which = next((n for n, known in enumerate(arrays) if known is array), len(arrays))
        if which == len(arrays):
            arrays.append(array)
        at.append((which, first))
    return arrays, at


def body(queries, keys, values, acc_out, acc_max, acc_sum, doc_lengths):
    rows, width = queries.shape
    heads = acc_max.shape[1]
    kv_heads = keys.shape[1] // HD
    group = heads // kv_heads
    n_outer = lax.axis_size("outer")
    n_inner = lax.axis_size("inner")
    if n_inner == 4:
        stages, early = STAGES, EARLY
    else:
        half = n_inner // 2
        stages, early = (tuple(range(half)), tuple(range(half, n_inner))), ()
    got = move(keys, values, n_outer, n_inner)
    ahead = pl.pallas_call(
        ahead_kernel,
        out_shape=jax.ShapeDtypeStruct((8, LANES), jnp.float32),
        out_specs=VMEM,
        compiler_params=pltpu.CompilerParams(vmem_limit_bytes=2**20),
        cost_estimate=pl.CostEstimate(flops=AHEAD_FLOPS, bytes_accessed=4096, transcendentals=0),
    )()
    stat = jax.ShapeDtypeStruct((heads, rows), jnp.float32)
    area = rows * rows * heads
    tile = jax.ShapeDtypeStruct((rows, LANES), jnp.bfloat16)

    def hide_of(steps):
        return jax.ShapeDtypeStruct((len(steps) * rows, LANES), jnp.bfloat16)

    ws, shrinks, late = [], [], []
    top, total = acc_max.T, acc_sum.T
    for at, steps in enumerate(stages):
        begin, end = at == 0, at + 1 == len(stages)
        now = early if begin else ()
        late.append([step for step in steps if step not in now])
        arrays, places = gather(got, [f"{step}k" for step in steps] + [f"{step}v" for step in now])
        operands = [doc_lengths, ahead, acc_out] if begin else [mine, hides[at - 1]]
        operands += [queries, top, total, *arrays]
        out_shape = [jax.ShapeDtypeStruct((max(1, len(late[-1])) * rows, heads * rows), jnp.bfloat16), stat, stat]
        out_shape += [stat] * ((not begin) + end)
        out_specs = [VMEM] * len(out_shape)
        if begin:
            out_shape.append(jax.ShapeDtypeStruct((width, rows), jnp.float32))
            out_shape += [jax.ShapeDtypeStruct((rows, width), jnp.bfloat16), stat, stat]
            out_specs += [VMEM] + [pl.BlockSpec(memory_space=pl.ANY)] * 3
            out_shape += [tile] + [hide_of(steps) for steps in stages[1:]] if not end else []
        outs = pl.pallas_call(
            functools.partial(
                weigh_kernel,
                stages,
                at,
                n_inner,
                len(now),
                places[: len(steps)],
                places[len(steps) :],
                kv_heads,
                group,
                1.0 / math.sqrt(HD),
            ),
            out_shape=tuple(out_shape),
            in_specs=([SMEM] if begin else [VMEM]) + [VMEM] * (len(operands) - 1),
            out_specs=tuple(out_specs + [VMEM] * (len(out_shape) - len(out_specs))),
            scratch_shapes=[pltpu.VMEM(x.shape, x.dtype) for x in (tile, hide_of(steps))] + [pltpu.SemaphoreType.DMA((3,))]
            if begin
            else [],
            compiler_params=pltpu.CompilerParams(vmem_limit_bytes=12 * 2**20),
            cost_estimate=pl.CostEstimate(
                flops=2 * area * HD * (len(steps) + len(now)), bytes_accessed=2**20, transcendentals=area * len(steps)
            ),
        )(*operands)
        outs = list(outs)
        ws.append(outs[0])
        top, total = outs[1:3]
        outs = outs[3:]
        if end:
            inverse = outs.pop(0)
        if not begin:
            shrinks.append(outs.pop(0))
        else:
            acc, rest, outs = outs[0], outs[1:4], outs[4:]
            mine, hides = (outs[0], outs[1:]) if not end else (None, None)
    arrays, places = gather(got, [f"{step}v" for held in late for step in held])
    places = iter(places)
    v_at = [[next(places) for step in held] for held in late]
    out, top, total = pl.pallas_call(
        functools.partial(mix_kernel, stages, v_at, kv_heads, group),
        out_shape=(jax.ShapeDtypeStruct((rows, width), jnp.bfloat16), stat, stat),
        in_specs=[pl.BlockSpec(memory_space=pl.ANY)] * 3 + [VMEM] * (2 * len(stages) + 3 + len(arrays)),
        input_output_aliases={0: 0, 1: 1, 2: 2},
        out_specs=(pl.BlockSpec(memory_space=pl.ANY),) * 3,
        scratch_shapes=[
            pltpu.VMEM((rows, width), jnp.bfloat16),
            pltpu.SemaphoreType.DMA((heads // FLUSH,)),
            pltpu.SemaphoreType.DMA((2,)),
        ],
        compiler_params=pltpu.CompilerParams(vmem_limit_bytes=12 * 2**20),
        cost_estimate=pl.CostEstimate(flops=2 * area * HD * n_inner, bytes_accessed=2**20, transcendentals=0),
    )(*rest, top, total, *ws, *shrinks, acc, inverse, *arrays)
    return out, top.T, total.T


def solution(mesh):
    split = P(("outer", "inner"), None)
    return jax.shard_map(
        body,
        mesh=mesh,
        in_specs=(split,) * 6 + (P(),),
        out_specs=(split,) * 3,
        check_vma=False,
    )
```

```python
import functools
import math

import jax
import jax.numpy as jnp
from jax import lax
from jax.experimental import pallas as pl
from jax.experimental.pallas import tpu as pltpu
from jax.sharding import PartitionSpec as P

HD = 128
LANES = 128
HIDE = -1e30
LOG2E = math.log2(math.e)
VMEM = pl.BlockSpec(memory_space=pltpu.VMEM)
SMEM = pl.BlockSpec(memory_space=pltpu.SMEM)
PAIR = 1
EARLY_PAIR = 4
MIX_PAIR = 2
FLUSH = 8
PLAN = (
    (("0k",), (), 0),
    (("1k",), (), 1),
    (("2k",), (), 2),
    (("0v",), (), 0),
    (("2v",), (), 2),
    (("3k",), ("1k",), 2),
    (("1v", "3v"), ("0v", "2v"), 1),
)
STAGES = ((0, 1), (2,), (3,))
EARLY = ((), (2,), ())
TIES = {}
AHEAD_FLOPS = 2 * 10**10


def source(at, step, n_inner):
    return at ^ step if n_inner & (n_inner - 1) == 0 else lax.rem(at + step, n_inner)


def ahead_kernel(out_ref):
    out_ref[...] = jnp.zeros_like(out_ref)


def masks(steps, n_inner, doc_ref, mine_ref, hide_refs):
    rows = mine_ref.shape[0]
    outer_at = lax.axis_index("outer")
    inner_at = lax.axis_index("inner")
    lane = lax.broadcasted_iota(jnp.int32, (8, LANES), 1)
    far = jnp.full((8, LANES), 2**30, jnp.int32)

    def one(d, state):
        first, starts, ends = state
        last = first + doc_ref[d]
        return last, jnp.where(lane == d, first, starts), jnp.where(lane == d, last, ends)

    unused, starts, ends = lax.fori_loop(0, doc_ref.shape[0], one, (jnp.int32(0), far, far), unroll=4)
    tok = lax.broadcasted_iota(jnp.int32, (rows, LANES), 0)
    qpos = tok + (outer_at * n_inner + inner_at) * rows
    mine_ref[...] = jnp.where((starts[:1] <= qpos) & (qpos < ends[:1]), 1.0, 0.0).astype(jnp.bfloat16)
    for hide_ref, held in zip(hide_refs, steps):
        for place, step in enumerate(held):
            kpos = tok + ((outer_at - 1) * n_inner + source(inner_at, step, n_inner)) * rows
            hide_ref[pl.ds(place * rows, rows), :] = jnp.where(kpos < starts[:1], HIDE, 0.0).astype(jnp.bfloat16)


def rows_of(ref, heads):
    return jnp.concatenate([ref[pl.ds(x, 1), :] for x in heads], axis=1)


def work_of(kv_heads, group, pair):
    return [(h, [h * group + g + k for k in range(pair)]) for h in range(kv_heads) for g in range(0, group, pair)]


def weigh_kernel(stages, at, n_inner, early, k_at, v_at, kv_heads, group, scale, *refs):
    begin, end = at == 0, at + 1 == len(stages)
    carry = begin or early > 0
    refs = list(refs)
    if begin:
        doc_ref, unused, old_ref = refs[:3]
        mine_ref, hide_ref = refs[-3:-1]
        refs = refs[3:-3] + refs[-1:]
    else:
        mine_ref, hide_ref = refs[:2]
        refs = refs[2:]
        if carry:
            old_ref = refs.pop(0)
    q_ref, max_ref, sum_ref = refs[:3]
    rows = q_ref.shape[0]
    k_refs = [refs[3 + which].at[pl.ds(first, rows)] for which, first in k_at]
    v_refs = [refs[3 + which].at[pl.ds(first, rows)] for which, first in v_at]
    refs = refs[3 + 1 + max(which for which, first in k_at + v_at) :]
    w_ref, top_ref, total_ref = refs[:3]
    refs = refs[3:]
    if end:
        inverse_ref = refs.pop(0)
    if not begin:
        shrink_ref = refs.pop(0)
    if carry:
        acc_ref = refs.pop(0)
    if begin:
        rest_refs = refs[:3]
        rest_sems, refs = refs[-1], refs[3:-1]
        if len(stages) > 1:
            later_mine_ref, later_refs = refs[0], refs[1:]
    split = early * rows
    pair = EARLY_PAIR if early else PAIR
    work = work_of(kv_heads, group, pair)
    live = lax.axis_index("outer") > 0

    def finish(heads, top, total, shrink, numer):
        inverse = 1.0 / total if end else None
        for k, x in enumerate(heads):
            cut = slice(k * rows, (k + 1) * rows)
            top_ref[pl.ds(x, 1), :] = top[:, cut]
            total_ref[pl.ds(x, 1), :] = total[:, cut]
            if end:
                inverse_ref[pl.ds(x, 1), :] = inverse[:, cut]
            if carry:
                acc_ref[pl.ds(x * HD, HD), :] = numer[:, cut]
            if not begin:
                shrink_ref[pl.ds(x, 1), :] = shrink[:, cut]

    def old_of(heads):
        if not begin:
            return jnp.concatenate([old_ref[pl.ds(x * HD, HD), :] for x in heads], axis=1)
        return jnp.concatenate([old_ref[:, pl.ds(x * HD, HD)].T for x in heads], axis=1).astype(jnp.float32)

    @pl.when(live)
    def _():
        if begin:
            masks(stages, n_inner, doc_ref, mine_ref, [hide_ref] + list(later_refs if len(stages) > 1 else []))
            if len(stages) > 1:
                later_mine_ref[...] = mine_ref[...]
        mine = jnp.concatenate([mine_ref[...]] * pair, axis=0)
        keys, vals = {}, {}

        def score(h, heads):
            if h not in keys:
                cols = pl.ds(h * HD, HD)
                keys[h] = jnp.concatenate([jnp.concatenate([k[:, cols] for k in k_refs], axis=0), hide_ref[...]], axis=1)
                vals[h] = jnp.concatenate([v[:, cols].T for v in v_refs], axis=1) if early else None
            q = jnp.concatenate([jnp.concatenate([q_ref[:, pl.ds(x * HD, HD)] for x in heads], axis=0), mine], axis=1)
            return lax.dot_general(keys[h], q, (((1,), (1,)), ((), ())), preferred_element_type=jnp.float32)

        def soften(s, heads):
            old_max = rows_of(max_ref, heads)
            top = jnp.maximum(old_max, jnp.max(s, axis=0, keepdims=True) * scale)
            w = jnp.exp2(s * (scale * LOG2E) - top * LOG2E)
            shrink = jnp.exp2((old_max - top) * LOG2E)
            kept = rows_of(sum_ref, heads) * shrink
            total = kept + jnp.sum(w, axis=0, keepdims=True)
            w = w.astype(jnp.bfloat16)
            if split < w.shape[0]:
                w_ref[:, pl.ds(heads[0] * rows, len(heads) * rows)] = w[split:]
            return kept, top, total, shrink, w[:split]

        def mix(h, heads, kept, top, total, shrink, w):
            numer = old_of(heads) * (kept if begin else shrink) if carry else None
            if early:
                numer += jnp.dot(vals[h], w, preferred_element_type=jnp.float32)
            finish(heads, top, total, shrink, numer)

        scores, soft = {}, {}
        for t in range(len(work) + 2):
            if t < len(work):
                scores[t] = score(*work[t])
            if 0 <= t - 1 < len(work):
                soft[t - 1] = soften(scores.pop(t - 1), work[t - 1][1])
            if 0 <= t - 2 < len(work):
                mix(*work[t - 2], *soft.pop(t - 2))

    @pl.when(jnp.logical_not(live))
    def _():
        if begin:
            copies = [
                pltpu.make_async_copy(ref, rest, rest_sems.at[n])
                for n, (ref, rest) in enumerate(zip((old_ref, max_ref, sum_ref), rest_refs))
            ]
            for copy in copies:
                copy.start()
        top_ref[...] = max_ref[...]
        total_ref[...] = sum_ref[...]
        if begin:
            for copy in copies:
                copy.wait()


def mix_kernel(carried, v_at, kv_heads, group, *refs):
    out_ref, top_out, total_out, stage, sems, stat_sems = refs[-6:]
    top_ref, total_ref = refs[3:5]
    refs = refs[5:]
    rows = out_ref.shape[0]
    count = len(v_at)
    stats = [
        pltpu.make_async_copy(top_ref, top_out, stat_sems.at[0]),
        pltpu.make_async_copy(total_ref, total_out, stat_sems.at[1]),
    ]
    w_refs, shrink_refs = refs[:count], refs[count : 2 * count - 1]
    acc_ref, inverse_ref = refs[2 * count - 1 : 2 * count + 1]
    refs = refs[2 * count + 1 :]
    v_refs = [[refs[which].at[pl.ds(first, rows)] for which, first in held] for held in v_at]
    wide = FLUSH * HD
    work = work_of(kv_heads, group, MIX_PAIR)

    def flush(h):
        span = pl.ds(h * wide, wide)
        return pltpu.make_async_copy(stage.at[:, span], out_ref.at[:, span], sems.at[h])

    def finish(heads, numer):
        result = (numer * rows_of(inverse_ref, heads)).astype(jnp.bfloat16)
        for k, x in enumerate(heads):
            stage[:, pl.ds(x * HD, HD)] = result[:, k * rows : (k + 1) * rows].T
        if (heads[-1] + 1) % FLUSH == 0:
            flush(heads[-1] // FLUSH).start()

    def numer_of(heads):
        return jnp.concatenate([acc_ref[pl.ds(x * HD, HD), :] for x in heads], axis=1)

    @pl.when(lax.axis_index("outer") > 0)
    def _():
        for copy in stats:
            copy.start()
        vals = {}

        def mixed(h, heads):
            if h not in vals:
                cols = pl.ds(h * HD, HD)
                vals[h] = [jnp.concatenate([v[:, cols].T for v in held], axis=1) if held else None for held in v_refs]
            at = pl.ds(heads[0] * rows, len(heads) * rows)
            return [
                jnp.dot(v, w[:, at], preferred_element_type=jnp.float32) if v is not None else None
                for v, w in zip(vals[h], w_refs)
            ]

        def close(heads, parts):
            numer = None
            for at, part in enumerate(parts):
                terms = [numer, numer_of(heads) if at == carried else None, part]
                numer = functools.reduce(lambda x, y: x + y, [term for term in terms if term is not None], jnp.float32(0.0))
                if at + 1 < len(parts):
                    numer = numer * rows_of(shrink_refs[at], heads)
            finish(heads, numer)

        held = {}
        for t in range(len(work) + 1):
            if t < len(work):
                held[t] = mixed(*work[t])
            if t >= 1:
                close(work[t - 1][1], held.pop(t - 1))

        for h in range(kv_heads * group // FLUSH):
            flush(h).wait()
        for copy in stats:
            copy.wait()


def move(keys, values, n_outer, n_inner):
    def direct(value, step):
        pairs = [
            (o * n_inner + (source(i, step, n_inner) if o + 1 < n_outer else i), (o + 1) % n_outer * n_inner + i)
            for o in range(n_outer)
            for i in range(n_inner)
        ]
        return lax.ppermute(value, ("outer", "inner"), pairs)

    def within(value, step):
        pairs = [
            (o * n_inner + (i ^ (step if o else 3 - step)), o * n_inner + i) for o in range(n_outer) for i in range(n_inner)
        ]
        return lax.ppermute(value, ("outer", "inner"), pairs)

    own = {"k": keys, "v": values}
    rows = keys.shape[0]
    got = {}
    if n_inner == 4:
        plan = PLAN
    else:
        plan = [((f"{step}{kind}",), (), step) for kind in "kv" for step in range(n_inner)]
    for pieces, taken, step in plan:
        after = [x for x in TIES.get(pieces[0], ()) if n_inner == 4]
        if taken:
            parts = [got[x][0][got[x][1] : got[x][1] + rows] if got[x][0].shape[0] > rows else got[x][0] for x in taken]
            sent = jnp.concatenate(parts, axis=0) if len(parts) > 1 else parts[0]
        else:
            sent = own[pieces[0][-1]]
        if after:
            held = lax.optimization_barrier((sent, *[got[x][0] for x in after]))
            sent = held[0]
            for x, array in zip(after, held[1:]):
                got[x] = (array, got[x][1])
        moved = within(sent, step) if taken else direct(sent, step)
        for place, piece in enumerate(pieces):
            got[piece] = (moved, place * rows)
    return got


def gather(got, pieces):
    arrays, at = [], []
    for piece in pieces:
        array, first = got[piece]
        which = next((n for n, known in enumerate(arrays) if known is array), len(arrays))
        if which == len(arrays):
            arrays.append(array)
        at.append((which, first))
    return arrays, at


def body(queries, keys, values, acc_out, acc_max, acc_sum, doc_lengths):
    rows, width = queries.shape
    heads = acc_max.shape[1]
    kv_heads = keys.shape[1] // HD
    group = heads // kv_heads
    n_outer = lax.axis_size("outer")
    n_inner = lax.axis_size("inner")
    if n_inner == 4:
        stages, early = STAGES, EARLY
    else:
        half = n_inner // 2
        stages, early = (tuple(range(half)), tuple(range(half, n_inner))), ((), ())
    got = move(keys, values, n_outer, n_inner)
    ahead = pl.pallas_call(
        ahead_kernel,
        out_shape=jax.ShapeDtypeStruct((8, LANES), jnp.float32),
        out_specs=VMEM,
        compiler_params=pltpu.CompilerParams(vmem_limit_bytes=2**20),
        cost_estimate=pl.CostEstimate(flops=AHEAD_FLOPS, bytes_accessed=4096, transcendentals=0),
    )()
    stat = jax.ShapeDtypeStruct((heads, rows), jnp.float32)
    area = rows * rows * heads
    tile = jax.ShapeDtypeStruct((rows, LANES), jnp.bfloat16)

    def hide_of(steps):
        return jax.ShapeDtypeStruct((len(steps) * rows, LANES), jnp.bfloat16)

    ws, shrinks, late = [], [], []
    top, total = acc_max.T, acc_sum.T
    for at, steps in enumerate(stages):
        begin, end = at == 0, at + 1 == len(stages)
        now = early[at]
        carry = begin or len(now) > 0
        late.append([step for step in steps if step not in now])
        order = (*now, *late[-1])
        arrays, places = gather(got, [f"{step}k" for step in order] + [f"{step}v" for step in now])
        operands = [doc_lengths, ahead, acc_out] if begin else [mine, hides[at - 1]] + ([acc] if carry else [])
        operands += [queries, top, total, *arrays]
        out_shape = [jax.ShapeDtypeStruct((max(1, len(late[-1])) * rows, heads * rows), jnp.bfloat16), stat, stat]
        out_shape += [stat] * ((not begin) + end)
        if carry:
            out_shape.append(jax.ShapeDtypeStruct((width, rows), jnp.float32))
        out_specs = [VMEM] * len(out_shape)
        if begin:
            out_shape += [jax.ShapeDtypeStruct((rows, width), jnp.bfloat16), stat, stat]
            out_specs += [pl.BlockSpec(memory_space=pl.ANY)] * 3
            out_shape += [tile] + [hide_of(held) for held in stages[1:]] if not end else []
        outs = pl.pallas_call(
            functools.partial(
                weigh_kernel,
                (order, *stages[1:]) if begin else stages,
                at,
                n_inner,
                len(now),
                places[: len(steps)],
                places[len(steps) :],
                kv_heads,
                group,
                1.0 / math.sqrt(HD),
            ),
            out_shape=tuple(out_shape),
            in_specs=([SMEM] if begin else [VMEM]) + [VMEM] * (len(operands) - 1),
            out_specs=tuple(out_specs + [VMEM] * (len(out_shape) - len(out_specs))),
            scratch_shapes=[pltpu.VMEM(x.shape, x.dtype) for x in (tile, hide_of(steps))] + [pltpu.SemaphoreType.DMA((3,))]
            if begin
            else [],
            compiler_params=pltpu.CompilerParams(vmem_limit_bytes=12 * 2**20),
            cost_estimate=pl.CostEstimate(
                flops=2 * area * HD * (len(steps) + len(now)), bytes_accessed=2**20, transcendentals=area * len(steps)
            ),
        )(*operands)
        outs = list(outs)
        ws.append(outs[0])
        top, total = outs[1:3]
        outs = outs[3:]
        if end:
            inverse = outs.pop(0)
        if not begin:
            shrinks.append(outs.pop(0))
        if carry:
            acc, carried = outs.pop(0), at
        if begin:
            rest, outs = outs[:3], outs[3:]
            mine, hides = (outs[0], outs[1:]) if not end else (None, None)
    arrays, places = gather(got, [f"{step}v" for held in late for step in held])
    places = iter(places)
    v_at = [[next(places) for step in held] for held in late]
    out, top, total = pl.pallas_call(
        functools.partial(mix_kernel, carried, v_at, kv_heads, group),
        out_shape=(jax.ShapeDtypeStruct((rows, width), jnp.bfloat16), stat, stat),
        in_specs=[pl.BlockSpec(memory_space=pl.ANY)] * 3 + [VMEM] * (2 * len(stages) + 3 + len(arrays)),
        input_output_aliases={0: 0, 1: 1, 2: 2},
        out_specs=(pl.BlockSpec(memory_space=pl.ANY),) * 3,
        scratch_shapes=[
            pltpu.VMEM((rows, width), jnp.bfloat16),
            pltpu.SemaphoreType.DMA((heads // FLUSH,)),
            pltpu.SemaphoreType.DMA((2,)),
        ],
        compiler_params=pltpu.CompilerParams(vmem_limit_bytes=12 * 2**20),
        cost_estimate=pl.CostEstimate(flops=2 * area * HD * n_inner, bytes_accessed=2**20, transcendentals=0),
    )(*rest, top, total, *ws, *shrinks, acc, inverse, *arrays)
    return out, top.T, total.T


def solution(mesh):
    split = P(("outer", "inner"), None)
    return jax.shard_map(
        body,
        mesh=mesh,
        in_specs=(split,) * 6 + (P(),),
        out_specs=(split,) * 3,
        check_vma=False,
    )
```

```python
import functools
import math

import jax
import jax.numpy as jnp
from jax import lax
from jax.experimental import pallas as pl
from jax.experimental.pallas import tpu as pltpu
from jax.sharding import PartitionSpec as P

HD = 128
LANES = 128
HIDE = -1e30
LOG2E = math.log2(math.e)
VMEM = pl.BlockSpec(memory_space=pltpu.VMEM)
SMEM = pl.BlockSpec(memory_space=pltpu.SMEM)
PAIR = 1
EARLY_PAIR = 4
MIX_PAIR = 2
FLUSH = 8
PLAN = (
    (("0k",), (), 0),
    (("1k",), (), 1),
    (("2k",), (), 2),
    (("0v",), (), 0),
    (("2v",), (), 2),
    (("3k",), ("1k",), 2),
    (("1v", "3v"), ("0v", "2v"), 1),
)
STAGES = ((0, 1), (2,), (3,))
EARLY = ((), (2,), ())
TIES = {}
AHEAD_FLOPS = 2 * 10**10


def source(at, step, n_inner):
    return at ^ step if n_inner & (n_inner - 1) == 0 else lax.rem(at + step, n_inner)


def ahead_kernel(out_ref):
    out_ref[...] = jnp.zeros_like(out_ref)


def masks(steps, n_inner, doc_ref, mine_ref, hide_refs):
    rows = mine_ref.shape[0]
    outer_at = lax.axis_index("outer")
    inner_at = lax.axis_index("inner")
    lane = lax.broadcasted_iota(jnp.int32, (8, LANES), 1)
    far = jnp.full((8, LANES), 2**30, jnp.int32)

    def one(d, state):
        first, starts, ends = state
        last = first + doc_ref[d]
        return last, jnp.where(lane == d, first, starts), jnp.where(lane == d, last, ends)

    unused, starts, ends = lax.fori_loop(0, doc_ref.shape[0], one, (jnp.int32(0), far, far), unroll=4)
    tok = lax.broadcasted_iota(jnp.int32, (rows, LANES), 0)
    qpos = tok + (outer_at * n_inner + inner_at) * rows
    mine_ref[...] = jnp.where((starts[:1] <= qpos) & (qpos < ends[:1]), 1.0, 0.0).astype(jnp.bfloat16)
    for hide_ref, held in zip(hide_refs, steps):
        for place, step in enumerate(held):
            kpos = tok + ((outer_at - 1) * n_inner + source(inner_at, step, n_inner)) * rows
            hide_ref[pl.ds(place * rows, rows), :] = jnp.where(kpos < starts[:1], HIDE, 0.0).astype(jnp.bfloat16)


def rows_of(ref, heads):
    return jnp.concatenate([ref[pl.ds(x, 1), :] for x in heads], axis=1)


def work_of(kv_heads, group, pair):
    return [(h, [h * group + g + k for k in range(pair)]) for h in range(kv_heads) for g in range(0, group, pair)]


def weigh_kernel(stages, at, n_inner, early, k_at, v_at, kv_heads, group, scale, *refs):
    begin, end = at == 0, at + 1 == len(stages)
    carry = begin or early > 0
    refs = list(refs)
    if begin:
        doc_ref, unused, old_ref = refs[:3]
        mine_ref, hide_ref = refs[-3:-1]
        refs = refs[3:-3] + refs[-1:]
    else:
        mine_ref, hide_ref = refs[:2]
        refs = refs[2:]
        if carry:
            old_ref = refs.pop(0)
    q_ref, max_ref, sum_ref = refs[:3]
    rows = q_ref.shape[0]
    k_refs = [refs[3 + which].at[pl.ds(first, rows)] for which, first in k_at]
    v_refs = [refs[3 + which].at[pl.ds(first, rows)] for which, first in v_at]
    refs = refs[3 + 1 + max(which for which, first in k_at + v_at) :]
    w_ref, top_ref, total_ref = refs[:3]
    refs = refs[3:]
    if end:
        inverse_ref = refs.pop(0)
    if not begin:
        shrink_ref = refs.pop(0)
    if carry:
        acc_ref = refs.pop(0)
    if begin:
        rest_refs = refs[:3]
        rest_sems, refs = refs[-1], refs[3:-1]
        if len(stages) > 1:
            later_mine_ref, later_refs = refs[0], refs[1:]
    split = early * rows
    pair = EARLY_PAIR if early else PAIR
    work = work_of(kv_heads, group, pair)
    live = lax.axis_index("outer") > 0

    def finish(heads, top, total, shrink, numer):
        inverse = 1.0 / total if end else None
        for k, x in enumerate(heads):
            cut = slice(k * rows, (k + 1) * rows)
            top_ref[pl.ds(x, 1), :] = top[:, cut]
            total_ref[pl.ds(x, 1), :] = total[:, cut]
            if end:
                inverse_ref[pl.ds(x, 1), :] = inverse[:, cut]
            if carry:
                acc_ref[pl.ds(x * HD, HD), :] = numer[:, cut]
            if not begin:
                shrink_ref[pl.ds(x, 1), :] = shrink[:, cut]

    def old_of(heads):
        if not begin:
            return jnp.concatenate([old_ref[pl.ds(x * HD, HD), :] for x in heads], axis=1)
        return jnp.concatenate([old_ref[:, pl.ds(x * HD, HD)].T for x in heads], axis=1).astype(jnp.float32)

    @pl.when(live)
    def _():
        if begin:
            masks(stages, n_inner, doc_ref, mine_ref, [hide_ref] + list(later_refs if len(stages) > 1 else []))
            if len(stages) > 1:
                later_mine_ref[...] = mine_ref[...]
        mine = jnp.concatenate([mine_ref[...]] * pair, axis=0)
        keys, vals = {}, {}

        def score(h, heads):
            if h not in keys:
                cols = pl.ds(h * HD, HD)
                keys[h] = jnp.concatenate([jnp.concatenate([k[:, cols] for k in k_refs], axis=0), hide_ref[...]], axis=1)
                vals[h] = jnp.concatenate([v[:, cols].T for v in v_refs], axis=1) if early else None
            q = jnp.concatenate([jnp.concatenate([q_ref[:, pl.ds(x * HD, HD)] for x in heads], axis=0), mine], axis=1)
            return lax.dot_general(keys[h], q, (((1,), (1,)), ((), ())), preferred_element_type=jnp.float32)

        def soften(s, heads):
            old_max = rows_of(max_ref, heads)
            top = jnp.maximum(old_max, jnp.max(s, axis=0, keepdims=True) * scale)
            w = jnp.exp2(s * (scale * LOG2E) - top * LOG2E)
            shrink = jnp.exp2((old_max - top) * LOG2E)
            kept = rows_of(sum_ref, heads) * shrink
            total = kept + jnp.sum(w, axis=0, keepdims=True)
            w = w.astype(jnp.bfloat16)
            if split < w.shape[0]:
                w_ref[:, pl.ds(heads[0] * rows, len(heads) * rows)] = w[split:]
            return kept, top, total, shrink, w[:split]

        def mix(h, heads, kept, top, total, shrink, w):
            numer = old_of(heads) * (kept if begin else shrink) if carry else None
            if early:
                numer += jnp.dot(vals[h], w, preferred_element_type=jnp.float32)
            finish(heads, top, total, shrink, numer)

        scores, soft = {}, {}
        for t in range(len(work) + 2):
            if t < len(work):
                scores[t] = score(*work[t])
            if 0 <= t - 1 < len(work):
                soft[t - 1] = soften(scores.pop(t - 1), work[t - 1][1])
            if 0 <= t - 2 < len(work):
                mix(*work[t - 2], *soft.pop(t - 2))

    @pl.when(jnp.logical_not(live))
    def _():
        if begin:
            copies = [
                pltpu.make_async_copy(ref, rest, rest_sems.at[n])
                for n, (ref, rest) in enumerate(zip((old_ref, max_ref, sum_ref), rest_refs))
            ]
            for copy in copies:
                copy.start()
        top_ref[...] = max_ref[...]
        total_ref[...] = sum_ref[...]
        if begin:
            for copy in copies:
                copy.wait()


def mix_kernel(carried, v_at, kv_heads, group, *refs):
    out_ref, top_out, total_out, stage, sems, stat_sems = refs[-6:]
    top_ref, total_ref = refs[3:5]
    refs = refs[5:]
    rows = out_ref.shape[0]
    count = len(v_at)
    stats = [
        pltpu.make_async_copy(top_ref, top_out, stat_sems.at[0]),
        pltpu.make_async_copy(total_ref, total_out, stat_sems.at[1]),
    ]
    w_refs, shrink_refs = refs[:count], refs[count : 2 * count - 1]
    acc_ref, inverse_ref = refs[2 * count - 1 : 2 * count + 1]
    refs = refs[2 * count + 1 :]
    v_refs = [[refs[which].at[pl.ds(first, rows)] for which, first in held] for held in v_at]
    wide = FLUSH * HD
    work = work_of(kv_heads, group, MIX_PAIR)

    def flush(h):
        span = pl.ds(h * wide, wide)
        return pltpu.make_async_copy(stage.at[:, span], out_ref.at[:, span], sems.at[h])

    def finish(heads, numer):
        result = (numer * rows_of(inverse_ref, heads)).astype(jnp.bfloat16)
        for k, x in enumerate(heads):
            stage[:, pl.ds(x * HD, HD)] = result[:, k * rows : (k + 1) * rows].T
        if (heads[-1] + 1) % FLUSH == 0:
            flush(heads[-1] // FLUSH).start()

    def numer_of(heads):
        return jnp.concatenate([acc_ref[pl.ds(x * HD, HD), :] for x in heads], axis=1)

    @pl.when(lax.axis_index("outer") > 0)
    def _():
        for copy in stats:
            copy.start()
        vals = {}

        def mixed(h, heads):
            if h not in vals:
                cols = pl.ds(h * HD, HD)
                vals[h] = [jnp.concatenate([v[:, cols].T for v in held], axis=1) if held else None for held in v_refs]
            at = pl.ds(heads[0] * rows, len(heads) * rows)
            return [
                jnp.dot(v, w[:, at], preferred_element_type=jnp.float32) if v is not None else None
                for v, w in zip(vals[h], w_refs)
            ]

        def close(heads, parts):
            numer = None
            for at, part in enumerate(parts):
                terms = [numer, numer_of(heads) if at == carried else None, part]
                numer = functools.reduce(lambda x, y: x + y, [term for term in terms if term is not None], jnp.float32(0.0))
                if at + 1 < len(parts):
                    numer = numer * rows_of(shrink_refs[at], heads)
            finish(heads, numer)

        held = {}
        for t in range(len(work) + 1):
            if t < len(work):
                held[t] = mixed(*work[t])
            if t >= 1:
                close(work[t - 1][1], held.pop(t - 1))

        for h in range(kv_heads * group // FLUSH):
            flush(h).wait()
        for copy in stats:
            copy.wait()


def move(keys, values, n_outer, n_inner):
    def direct(value, step):
        pairs = [
            (o * n_inner + (source(i, step, n_inner) if o + 1 < n_outer else i), (o + 1) % n_outer * n_inner + i)
            for o in range(n_outer)
            for i in range(n_inner)
        ]
        return lax.ppermute(value, ("outer", "inner"), pairs)

    def within(value, step):
        pairs = [
            (o * n_inner + (i ^ (step if o else 3 - step)), o * n_inner + i) for o in range(n_outer) for i in range(n_inner)
        ]
        return lax.ppermute(value, ("outer", "inner"), pairs)

    own = {"k": keys, "v": values}
    rows = keys.shape[0]
    got = {}
    if n_inner == 4:
        plan = PLAN
    else:
        plan = [((f"{step}{kind}",), (), step) for kind in "kv" for step in range(n_inner)]
    for pieces, taken, step in plan:
        after = [x for x in TIES.get(pieces[0], ()) if n_inner == 4]
        if taken:
            parts = [got[x][0][got[x][1] : got[x][1] + rows] if got[x][0].shape[0] > rows else got[x][0] for x in taken]
            sent = jnp.concatenate(parts, axis=0) if len(parts) > 1 else parts[0]
        else:
            sent = own[pieces[0][-1]]
        if after:
            held = lax.optimization_barrier((sent, *[got[x][0] for x in after]))
            sent = held[0]
            for x, array in zip(after, held[1:]):
                got[x] = (array, got[x][1])
        moved = within(sent, step) if taken else direct(sent, step)
        for place, piece in enumerate(pieces):
            got[piece] = (moved, place * rows)
    return got


def gather(got, pieces):
    arrays, at = [], []
    for piece in pieces:
        array, first = got[piece]
        which = next((n for n, known in enumerate(arrays) if known is array), len(arrays))
        if which == len(arrays):
            arrays.append(array)
        at.append((which, first))
    return arrays, at


def body(queries, keys, values, acc_out, acc_max, acc_sum, doc_lengths):
    rows, width = queries.shape
    heads = acc_max.shape[1]
    kv_heads = keys.shape[1] // HD
    group = heads // kv_heads
    n_outer = lax.axis_size("outer")
    n_inner = lax.axis_size("inner")
    if n_inner == 4:
        stages, early = STAGES, EARLY
    else:
        half = n_inner // 2
        stages, early = (tuple(range(half)), tuple(range(half, n_inner))), ((), ())
    got = move(keys, values, n_outer, n_inner)
    ahead = pl.pallas_call(
        ahead_kernel,
        out_shape=jax.ShapeDtypeStruct((8, LANES), jnp.float32),
        out_specs=VMEM,
        compiler_params=pltpu.CompilerParams(vmem_limit_bytes=2**20),
        cost_estimate=pl.CostEstimate(flops=AHEAD_FLOPS, bytes_accessed=4096, transcendentals=0),
    )()
    stat = jax.ShapeDtypeStruct((heads, rows), jnp.float32)
    area = rows * rows * heads
    tile = jax.ShapeDtypeStruct((rows, LANES), jnp.bfloat16)

    def hide_of(steps):
        return jax.ShapeDtypeStruct((len(steps) * rows, LANES), jnp.bfloat16)

    ws, shrinks, late = [], [], []
    top, total = acc_max.T, acc_sum.T
    for at, steps in enumerate(stages):
        begin, end = at == 0, at + 1 == len(stages)
        now = early[at]
        carry = begin or len(now) > 0
        late.append([step for step in steps if step not in now])
        order = (*now, *late[-1])
        arrays, places = gather(got, [f"{step}k" for step in order] + [f"{step}v" for step in now])
        operands = [doc_lengths, ahead, acc_out] if begin else [mine, hides[at - 1]] + ([acc] if carry else [])
        operands += [queries, top, total, *arrays]
        out_shape = [jax.ShapeDtypeStruct((max(1, len(late[-1])) * rows, heads * rows), jnp.bfloat16), stat, stat]
        out_shape += [stat] * ((not begin) + end)
        if carry:
            out_shape.append(jax.ShapeDtypeStruct((width, rows), jnp.float32))
        out_specs = [VMEM] * len(out_shape)
        if begin:
            out_shape += [jax.ShapeDtypeStruct((rows, width), jnp.bfloat16), stat, stat]
            out_specs += [pl.BlockSpec(memory_space=pl.ANY)] * 3
            out_shape += [tile] + [hide_of(held) for held in stages[1:]] if not end else []
        outs = pl.pallas_call(
            functools.partial(
                weigh_kernel,
                (order, *stages[1:]) if begin else stages,
                at,
                n_inner,
                len(now),
                places[: len(steps)],
                places[len(steps) :],
                kv_heads,
                group,
                1.0 / math.sqrt(HD),
            ),
            out_shape=tuple(out_shape),
            in_specs=([SMEM] if begin else [VMEM]) + [VMEM] * (len(operands) - 1),
            out_specs=tuple(out_specs + [VMEM] * (len(out_shape) - len(out_specs))),
            scratch_shapes=[pltpu.VMEM(x.shape, x.dtype) for x in (tile, hide_of(steps))] + [pltpu.SemaphoreType.DMA((3,))]
            if begin
            else [],
            compiler_params=pltpu.CompilerParams(vmem_limit_bytes=12 * 2**20),
            cost_estimate=pl.CostEstimate(
                flops=8 * area * HD * (len(steps) + len(now)), bytes_accessed=2**20, transcendentals=area * len(steps)
            ),
        )(*operands)
        outs = list(outs)
        ws.append(outs[0])
        top, total = outs[1:3]
        outs = outs[3:]
        if end:
            inverse = outs.pop(0)
        if not begin:
            shrinks.append(outs.pop(0))
        if carry:
            acc, carried = outs.pop(0), at
        if begin:
            rest, outs = outs[:3], outs[3:]
            mine, hides = (outs[0], outs[1:]) if not end else (None, None)
    arrays, places = gather(got, [f"{step}v" for held in late for step in held])
    places = iter(places)
    v_at = [[next(places) for step in held] for held in late]
    out, top, total = pl.pallas_call(
        functools.partial(mix_kernel, carried, v_at, kv_heads, group),
        out_shape=(jax.ShapeDtypeStruct((rows, width), jnp.bfloat16), stat, stat),
        in_specs=[pl.BlockSpec(memory_space=pl.ANY)] * 3 + [VMEM] * (2 * len(stages) + 3 + len(arrays)),
        input_output_aliases={0: 0, 1: 1, 2: 2},
        out_specs=(pl.BlockSpec(memory_space=pl.ANY),) * 3,
        scratch_shapes=[
            pltpu.VMEM((rows, width), jnp.bfloat16),
            pltpu.SemaphoreType.DMA((heads // FLUSH,)),
            pltpu.SemaphoreType.DMA((2,)),
        ],
        compiler_params=pltpu.CompilerParams(vmem_limit_bytes=12 * 2**20),
        cost_estimate=pl.CostEstimate(flops=2 * area * HD * n_inner, bytes_accessed=2**20, transcendentals=0),
    )(*rest, top, total, *ws, *shrinks, acc, inverse, *arrays)
    return out, top.T, total.T


def solution(mesh):
    split = P(("outer", "inner"), None)
    return jax.shard_map(
        body,
        mesh=mesh,
        in_specs=(split,) * 6 + (P(),),
        out_specs=(split,) * 3,
        check_vma=False,
    )
```
